32 devices in a mesh: span: 8 (over z, core), chord: 4 (over y, x).
Axes of the slice: x: 2, y: 2, z: 4, core: 2. Of those that a mesh axis runs over, the one named last changes fastest.
Arguments:
- right_side: float32 [16, 256, 512], P(None, 'span', 'chord'), may hold values from -6 to 6
- stiff_scale: float32 [256, 512], P('span', 'chord'), may hold values from 0.5 to 2
- extra_diag: float32 [256, 512], P('span', 'chord'), may hold values from 0.5 to 4
- iface_line: int32 [32], P('chord'), may hold values from 0 to 127, as said below
- partner: int32 [32], P('chord'), may hold values from 0 to 31, as said below
Outputs:
- solution: float32 [16, 256, 512], P(None, 'span', 'chord')
- residual: float32 [16, 256, 512], P(None, 'span', 'chord')
The draws below stay inside these ranges and needn't reach their ends.
Inputs may be any that keep to these rules, and one draw needn't show every extreme that they name: `iface_line`: each device's 8 entries are distinct; the first two are 0 and 127, the patch's edge lines. partner pairs the slots: partner[partner[q]] = q and partner[q] != q.
All inputs are finite; a program needn't handle non-finite values.
Results may differ from the reference program's by a relative error of at most 0.00016.
Values sent between devices are 32-bit elements; how exact they have to be, the bound alone decides.
A program may use at most 64 MiB of HBM per device.

```python
import math
import jax
import jax.numpy as jnp
from jax import lax

CC = 128
COLS = 16
IFACE = 8
ITERS = 2
NS = 256
NC = 512
SLOTS = 32


def draw_iface_line(key, part):
    device_keys = jax.random.split(jax.random.fold_in(key, 17), SLOTS // IFACE)

    def choose_lines(subkey):
        inner = jax.random.permutation(subkey, CC - 2)[:IFACE - 2].astype(jnp.int32) + 1
        edges = jnp.array([0, CC - 1], dtype=jnp.int32)
        return jnp.concatenate([edges, inner])
    return jax.vmap(choose_lines)(device_keys).reshape(SLOTS).astype(jnp.int32)


def draw_partner(key, part):
    shuffled = jax.random.permutation(jax.random.fold_in(key, 29), SLOTS).astype(jnp.int32)
    swapped = shuffled.reshape(-1, 2)[:, ::-1].reshape(-1)
    return jnp.zeros((SLOTS,), jnp.int32).at[shuffled].set(swapped)


def steps_of(own_key, extent, cuts, least, high):
    gain, own = 1.0, jax.random.fold_in(own_key, 6)
    for axis_at, blocks in cuts:
        draws = jnp.exp(jax.random.uniform(jax.random.fold_in(own, axis_at), (blocks,), jnp.float32, least / len(cuts), high / len(cuts)))
        gain = gain * jnp.repeat(draws, extent[axis_at] // blocks).reshape([-1 if axis == axis_at else 1 for axis in range(len(extent))])
    return gain


def bell_draw(key, extent, deviation, most, shards=(), kind=jnp.bfloat16):
    result = deviation * jax.random.normal(key, extent, jnp.float32)
    if shards:
        result = result * steps_of(key, extent, shards, -0.22, 0.18)
    return jnp.clip(result, -most, most).astype(kind)


def setup_inputs(seed: int = 0) -> dict:
    arg_keys = jax.random.split(jax.random.key(seed), 6)
    return {
        "right_side": bell_draw(arg_keys[0], (COLS, NS, NC), 1.0, 6.0, ((1, 8), (2, 4)), jnp.float32),
        "stiff_scale": jnp.clip(jnp.exp(math.log(2.0) - 1.3862944 * jax.random.uniform(arg_keys[1], (NS, NC), jnp.float32) ** steps_of(arg_keys[1], (NS, NC), ((0, 8), (1, 4)), -0.2, 0.2)), 0.5, 2.0),
        "extra_diag": jnp.clip(jnp.exp(math.log(4.0) - 2.0794415 * jax.random.uniform(arg_keys[2], (NS, NC), jnp.float32) ** steps_of(arg_keys[2], (NS, NC), ((0, 8), (1, 4)), -0.2, 0.2)), 0.5, 4.0),
        "iface_line": draw_iface_line(jax.random.fold_in(arg_keys[5], 71), 0),
        "partner": draw_partner(jax.random.fold_in(arg_keys[5], 71), 0),
    }


mass_taps = (1.0 / 5040.0, 120.0 / 5040.0, 1191.0 / 5040.0, 2416.0 / 5040.0, 1191.0 / 5040.0, 120.0 / 5040.0, 1.0 / 5040.0)
bend_taps = (1.0 / 6.0, 0.0, -1.5, 8.0 / 3.0, -1.5, 0.0, 1.0 / 6.0)
penalty_weight = 4.0

def tap_sum(extended, tap_list, along_dim, length):
    summed = tap_list[0] * lax.slice_in_dim(extended, 0, length, axis=along_dim)
    for offset in range(1, 7):
        if tap_list[offset] != 0.0:
            summed = summed + tap_list[offset] * lax.slice_in_dim(extended, offset, offset + length, axis=along_dim)
    return summed

def gram_of(left_field, right_field):
    return jnp.dot(left_field.reshape(left_field.shape[0], -1), right_field.reshape(right_field.shape[0], -1).T, precision=lax.Precision.HIGHEST)

def combine(vector, coeffs):
    return jnp.einsum('aij,ab->bij', vector, coeffs, precision=lax.Precision.HIGHEST)

def spd_solve(matrix, right_hand):
    factor = jnp.linalg.cholesky(matrix)
    forward = lax.linalg.triangular_solve(factor, right_hand, left_side=True, lower=True)
    return lax.linalg.triangular_solve(factor, forward, left_side=True, lower=True, transpose_a=True)

def stiffness(vector, stiff_scale, extra_diag, iface_line, partner):

    def one_column(column):
        weighted = stiff_scale * column
        wrapped = jnp.concatenate([weighted[:, -3:], weighted, weighted[:, :3]], axis=1)
        chord_mass = tap_sum(wrapped, mass_taps, 1, NC)
        chord_bend = tap_sum(wrapped, bend_taps, 1, NC)
        zero_rim = jnp.zeros((3, NC), column.dtype)
        mass_ext = jnp.concatenate([zero_rim, chord_mass, zero_rim], axis=0)
        bend_ext = jnp.concatenate([zero_rim, chord_bend, zero_rim], axis=0)
        spanwise = tap_sum(mass_ext, bend_taps, 0, NS) + tap_sum(bend_ext, mass_taps, 0, NS)
        return stiff_scale * spanwise + extra_diag * column
    stiff_part = lax.map(one_column, vector)
    slot_ids = jnp.arange(SLOTS, dtype=jnp.int32)
    global_line = slot_ids // IFACE * CC + iface_line.astype(jnp.int32)
    own_values = vector[:, :, global_line]
    partner_values = own_values[:, :, partner.astype(jnp.int32)]
    return stiff_part.at[:, :, global_line].add(penalty_weight * (own_values - partner_values))

def reference(right_side, stiff_scale, extra_diag, iface_line, partner):
    solution = jnp.zeros_like(right_side)
    residual = right_side
    direction = right_side
    norm_now = gram_of(residual, residual)
    for iteration in range(ITERS):
        image_now = stiffness(direction, stiff_scale, extra_diag, iface_line, partner)
        curvature = gram_of(direction, image_now)
        alpha = spd_solve(curvature, norm_now)
        solution = solution + combine(direction, alpha)
        residual = residual - combine(image_now, alpha)
        if iteration + 1 < ITERS:
            norm_next = gram_of(residual, residual)
            beta = spd_solve(norm_now, norm_next)
            direction = residual + combine(direction, beta)
            norm_now = norm_next
    return (solution, residual)
```

```python
import functools

import jax
import jax.numpy as jnp
from jax import lax
from jax.experimental import pallas as pl
from jax.experimental.pallas import tpu as pltpu
from jax.sharding import PartitionSpec as P

mass_taps = (
    1.0 / 5040.0,
    120.0 / 5040.0,
    1191.0 / 5040.0,
    2416.0 / 5040.0,
    1191.0 / 5040.0,
    120.0 / 5040.0,
    1.0 / 5040.0,
)
bend_taps = (1.0 / 6.0, 0.0, -1.5, 8.0 / 3.0, -1.5, 0.0, 1.0 / 6.0)
penalty_weight = 4.0
REACH = 3
LANES = 128
TILE = 8
F32 = jnp.float32
MESH = pl.DeviceIdType.MESH


def dot(a, b, a_dim, b_dim):
    return lax.dot_general(
        a,
        b,
        (((a_dim,), (b_dim,)), ((), ())),
        precision=lax.Precision.HIGHEST,
        preferred_element_type=F32,
    )


def iota(shape, dim):
    return lax.broadcasted_iota(jnp.int32, shape, dim)


def taps_at(offset, taps):
    out = jnp.zeros(offset.shape, F32)
    for o in range(-REACH, REACH + 1):
        if taps[o + REACH] != 0.0:
            out = jnp.where(offset == o, F32(taps[o + REACH]), out)
    return out


def span_sum(ext_ref, taps, rows):
    total = F32(taps[REACH]) * ext_ref[REACH : REACH + rows]
    for o in range(1, REACH + 1):
        if taps[REACH + o] != 0.0:
            pair = ext_ref[REACH - o : REACH - o + rows] + ext_ref[REACH + o : REACH + o + rows]
            total = total + F32(taps[REACH + o]) * pair
    return total


def eliminate(table, first, count):
    row_at = iota(table.shape, 0)
    for k in range(count):
        column = table[:, first + k : first + k + 1]
        row = table[k : k + 1, :] / column[k : k + 1, :]
        table = jnp.where(row_at == k, row, table - column * row)
    return table


def kernel(
    n,
    N,
    right_ref,
    scale_ref,
    extra_ref,
    line_ref,
    partner_ref,
    solution_ref,
    residual_ref,
    basis,
    weighted,
    halo_out,
    halo,
    iface,
    rim,
    corner,
    ext_m,
    ext_b,
    early_c,
    early_s,
    late_c,
    late_s,
    rim_sems,
    halo_sems,
    corner_sems,
    iface_sems,
    chord_sems,
    span_sems,
):
    C, R, L = right_ref.shape
    RC = R * C
    slots = line_ref.shape[0]
    s = lax.axis_index("span")
    c = lax.axis_index("chord")
    right, left = lax.rem(c + 1, n), lax.rem(c + n - 1, n)
    above, below = s > 0, s < N - 1

    barrier = pltpu.get_barrier_semaphore()
    for d in range(1, n):
        pl.semaphore_signal(barrier, inc=1, device_id=(s, lax.rem(c + d, n)), device_id_type=MESH)
    for d in range(1, N):
        pl.semaphore_signal(barrier, inc=1, device_id=(lax.rem(s + d, N), c), device_id_type=MESH)

    @pl.when(above)
    def _():
        for side in (left, right):
            pl.semaphore_signal(barrier, inc=1, device_id=(s - 1, side), device_id_type=MESH)

    @pl.when(below)
    def _():
        for side in (left, right):
            pl.semaphore_signal(barrier, inc=1, device_id=(s + 1, side), device_id_type=MESH)

    @pl.when(jnp.logical_not(above))
    def _():
        for t in range(2):
            rim[t, 0] = jnp.zeros(rim.shape[2:], F32)
            corner[t, 0] = jnp.zeros(corner.shape[2:], F32)

    @pl.when(jnp.logical_not(below))
    def _():
        for t in range(2):
            rim[t, 1] = jnp.zeros(rim.shape[2:], F32)
            corner[t, 1] = jnp.zeros(corner.shape[2:], F32)

    offset = iota((L, L), 0) - iota((L, L), 1)
    band = jnp.concatenate([taps_at(offset, mass_taps), taps_at(offset, bend_taps)], axis=1)
    k_at, c_at = iota((2 * TILE, L), 0), iota((2 * TILE, L), 1)
    from_left = jnp.logical_and(k_at >= REACH, k_at < 2 * REACH)
    from_right = jnp.logical_and(k_at >= TILE, k_at < TILE + REACH)
    place = jnp.where(k_at < TILE, k_at - 2 * REACH, L + k_at - TILE)
    reach = jnp.where(jnp.logical_or(from_left, from_right), place - c_at, 2 * L)
    side_band = jnp.concatenate([taps_at(reach, mass_taps), taps_at(reach, bend_taps)], axis=1)
    h_at, hc_at = iota((TILE, L), 0), iota((TILE, L), 1)
    halo_line = jnp.where(h_at < REACH, h_at, L - 2 * REACH + h_at)
    halo_pick = jnp.where(
        jnp.logical_and(h_at < 2 * REACH, halo_line == hc_at), F32(1.0), F32(0.0)
    )

    q_at, qc_at = iota((slots, L), 0), iota((slots, L), 1)
    j_at, jc_at = iota((n * slots, L), 0), iota((n * slots, L), 1)
    pick = jnp.zeros((slots, L), F32)
    spread = jnp.zeros((n * slots, L), F32)
    for q in range(slots):
        line, mate = line_ref[q], partner_ref[q]
        pick = jnp.where(jnp.logical_and(q_at == q, qc_at == line), F32(1.0), pick)
        owner = lax.div(mate, jnp.int32(slots))
        away = c - owner
        away = jnp.where(away < 0, away + n, away)
        at = away * slots + (mate - owner * slots)
        spread = jnp.where(jnp.logical_and(j_at == at, jc_at == line), F32(-penalty_weight), spread)
    on_line = jnp.sum(pick, axis=0, keepdims=True)

    scale = scale_ref[...][:, None, :]
    diag = (extra_ref[...] + F32(penalty_weight) * on_line)[:, None, :]

    basis[0] = jnp.swapaxes(right_ref[...], 0, 1)

    def remote(src, dst, sems, at, to):
        return pltpu.make_async_remote_copy(
            src_ref=src,
            dst_ref=dst,
            send_sem=sems.at[(0,) + at],
            recv_sem=sems.at[(1,) + at],
            device_id=to,
            device_id_type=MESH,
        )

    def flat(t):
        return basis[t].reshape(RC, L)

    def wide(t):
        return jnp.concatenate([basis[t, r] for r in range(R)], axis=1)

    def copies(t):
        down = [remote(weighted.at[t, pl.ds(R - REACH, REACH)], rim.at[t, 0], rim_sems, (t, 0), (s + 1, c))]
        up = [remote(weighted.at[t, pl.ds(0, REACH)], rim.at[t, 1], rim_sems, (t, 1), (s - 1, c))]
        last, first = pl.ds(RC - LANES, LANES), pl.ds(0, LANES)
        for k, to in enumerate((right, left)):
            spot = pl.ds(k * TILE, TILE)
            down.append(
                remote(halo_out.at[t, :, last], corner.at[t, 0, spot], corner_sems, (t, 0, k), (s + 1, to))
            )
            up.append(
                remote(halo_out.at[t, :, first], corner.at[t, 1, spot], corner_sems, (t, 1, k), (s - 1, to))
            )
        around = []
        for k, to in enumerate((right, left)):
            spot = pl.ds(k * TILE, TILE)
            around.append(remote(halo_out.at[t], halo.at[t, spot], halo_sems, (t, k), (s, to)))
        for d in range(1, n):
            around.append(
                remote(
                    iface.at[t, pl.ds(0, slots)],
                    iface.at[t, pl.ds(d * slots, slots)],
                    iface_sems,
                    (t, d),
                    (s, lax.rem(c + d, n)),
                )
            )
        return down, up, around

    def prepare(t):
        w = scale * basis[t]
        weighted[t] = w
        halo_out[t] = dot(halo_pick, w.reshape(RC, L), 1, 1)
        iface[t, 0:slots] = dot(pick, flat(t), 1, 1)

    def send(t):
        down, up, around = copies(t)

        @pl.when(below)
        def _():
            for copy in down:
                copy.start()

        @pl.when(above)
        def _():
            for copy in up:
                copy.start()

        for copy in around:
            copy.start()

    def inner(t):
        both = dot(weighted[t].reshape(RC, L), band, 1, 0)
        ext_m[REACH : REACH + R] = both[:, :L].reshape(R, C, L)
        ext_b[REACH : REACH + R] = both[:, L:].reshape(R, C, L)

    def receive(t):
        down, up, around = copies(t)

        @pl.when(above)
        def _():
            for copy in down:
                copy.wait_recv()

        @pl.when(below)
        def _():
            for copy in up:
                copy.wait_recv()

        for copy in around:
            copy.wait_recv()

    def sent(t):
        down, up, around = copies(t)

        @pl.when(below)
        def _():
            for copy in down:
                copy.wait_send()

        @pl.when(above)
        def _():
            for copy in up:
                copy.wait_send()

        for copy in around:
            copy.wait_send()

    def outer(t):
        edge = REACH * C
        ends = dot(rim[t].reshape(2 * edge, L), band, 1, 0)
        top = ends[:edge] + dot(corner[t, 0], side_band, 0, 0)[LANES - edge :]
        low = ends[edge:] + dot(corner[t, 1], side_band, 0, 0)[:edge]
        mid = dot(halo[t], side_band, 0, 0)
        ext_m[0:REACH] = top[:, :L].reshape(REACH, C, L)
        ext_b[0:REACH] = top[:, L:].reshape(REACH, C, L)
        ext_m[REACH + R :] = low[:, :L].reshape(REACH, C, L)
        ext_b[REACH + R :] = low[:, L:].reshape(REACH, C, L)
        ext_m[REACH : REACH + R] += mid[:, :L].reshape(R, C, L)
        ext_b[REACH : REACH + R] += mid[:, L:].reshape(R, C, L)
        y = span_sum(ext_m, bend_taps, R) + span_sum(ext_b, mass_taps, R)
        coupled = dot(iface[t], spread, 0, 0).reshape(R, C, L)
        basis[t + 1] = scale * y + diag * basis[t] + coupled

    def group_copies(buf, sems, which, count, to):
        return [remote(buf.at[0], buf.at[d], sems, (which, d), to(d)) for d in range(1, count)]

    def along_chord(d):
        return (s, lax.rem(c + d, n))

    def along_span(d):
        return (lax.rem(s + d, N), c)

    def total(buf, count):
        out = buf[0]
        for d in range(1, count):
            out = out + buf[d]
        return out

    def pad(x):
        return jnp.concatenate([x, jnp.zeros((x.shape[0], LANES - x.shape[1]), F32)], axis=1)

    ec = group_copies(early_c, chord_sems, 0, n, along_chord)
    es = group_copies(early_s, span_sems, 0, N, along_span)
    lc = group_copies(late_c, chord_sems, 1, n, along_chord)
    ls = group_copies(late_s, span_sems, 1, N, along_span)

    prepare(0)
    greeted = (n - 1) + (N - 1) + 2 * (above.astype(jnp.int32) + below.astype(jnp.int32))
    pl.semaphore_wait(barrier, greeted)
    send(0)
    inner(0)
    receive(0)
    outer(0)
    prepare(1)
    send(1)

    v0, v1 = wide(0), wide(1)
    first = dot(v0, jnp.concatenate([v1, v0], axis=0), 1, 1)
    g11 = dot(v1, v1, 1, 1)
    early_c[0] = pad(jnp.concatenate([first[:, :C], g11, first[:, C:]], axis=1))
    for copy in ec:
        copy.start()
    inner(1)
    for copy in ec:
        copy.wait_recv()
    early_s[0] = total(early_c, n)
    for copy in es:
        copy.start()
    receive(1)
    outer(1)
    late_c[0] = pad(dot(wide(1), jnp.concatenate([wide(0), wide(2)], axis=0), 1, 1))
    for copy in lc:
        copy.start()
    for copy in es:
        copy.wait_recv()
    table = total(early_s, N)
    g01, g11 = table[:, :C], table[:, C : 2 * C]
    table = eliminate(table, 0, C)
    folded = dot(g11, table, 1, 0)
    slope = table[:, C : 2 * C]
    step = table[:, 2 * C : 3 * C]
    lead = pad(jnp.concatenate([jnp.zeros((C, 2 * C), F32), g01], axis=1))
    rest = lead - folded
    for copy in lc:
        copy.wait_recv()
    late_s[0] = total(late_c, n)
    for copy in ls:
        copy.start()
    for copy in ls:
        copy.wait_recv()
    table = eliminate(rest + total(late_s, N), C, C)
    y1 = table[:, 2 * C : 3 * C]
    y0 = step - dot(slope, y1, 1, 0)
    mix = jnp.concatenate([y0, y1], axis=0)

    v0, v1, v2 = wide(0), wide(1), wide(2)
    found = dot(mix, jnp.concatenate([v0, v1], axis=0), 0, 0)
    left_over = v0 - dot(mix, jnp.concatenate([v1, v2], axis=0), 0, 0)

    def narrow(x):
        rows = jnp.stack([x[:, r * L : (r + 1) * L] for r in range(R)], axis=0)
        return jnp.swapaxes(rows, 0, 1)

    solution_ref[...] = narrow(found)
    residual_ref[...] = narrow(left_over)
    sent(0)
    sent(1)
    for copy in ec + es + lc + ls:
        copy.wait_send()


def body(n, N, right_side, stiff_scale, extra_diag, iface_line, partner):
    C, R, L = right_side.shape
    slots = iface_line.shape[0]
    vmem = pl.BlockSpec(memory_space=pltpu.VMEM)
    smem = pl.BlockSpec(memory_space=pltpu.SMEM)
    dma = pltpu.SemaphoreType.DMA
    field = jax.ShapeDtypeStruct((C, R, L), F32)
    return pl.pallas_call(
        functools.partial(kernel, n, N),
        out_shape=(field, field),
        in_specs=[vmem, vmem, vmem, smem, smem],
        out_specs=(vmem, vmem),
        scratch_shapes=[
            pltpu.VMEM((3, R, C, L), F32),
            pltpu.VMEM((2, R, C, L), F32),
            pltpu.VMEM((2, TILE, R * C), F32),
            pltpu.VMEM((2, 2 * TILE, R * C), F32),
            pltpu.VMEM((2, n * slots, R * C), F32),
            pltpu.VMEM((2, 2, REACH, C, L), F32),
            pltpu.VMEM((2, 2, 2 * TILE, LANES), F32),
            pltpu.VMEM((R + 2 * REACH, C, L), F32),
            pltpu.VMEM((R + 2 * REACH, C, L), F32),
            pltpu.VMEM((n, C, LANES), F32),
            pltpu.VMEM((N, C, LANES), F32),
            pltpu.VMEM((n, C, LANES), F32),
            pltpu.VMEM((N, C, LANES), F32),
            dma((2, 2, 2)),
            dma((2, 2, 2)),
            dma((2, 2, 2, 2)),
            dma((2, 2, n)),
            dma((2, 2, n)),
            dma((2, 2, N)),
        ],
        compiler_params=pltpu.CompilerParams(
            collective_id=0, has_side_effects=True, vmem_limit_bytes=32 * 1024 * 1024
        ),
        name="shell_cg",
    )(right_side, stiff_scale, extra_diag, iface_line, partner)


def solution(mesh):
    sizes = dict(mesh.shape)
    return jax.shard_map(
        functools.partial(body, sizes["chord"], sizes["span"]),
        mesh=mesh,
        in_specs=(
            P(None, "span", "chord"),
            P("span", "chord"),
            P("span", "chord"),
            P("chord"),
            P("chord"),
        ),
        out_specs=(P(None, "span", "chord"), P(None, "span", "chord")),
        check_vma=False,
    )
```

```python
import functools

import jax
import jax.numpy as jnp
from jax import lax
from jax.experimental import pallas as pl
from jax.experimental.pallas import tpu as pltpu
from jax.sharding import PartitionSpec as P

mass_taps = (
    1.0 / 5040.0,
    120.0 / 5040.0,
    1191.0 / 5040.0,
    2416.0 / 5040.0,
    1191.0 / 5040.0,
    120.0 / 5040.0,
    1.0 / 5040.0,
)
bend_taps = (1.0 / 6.0, 0.0, -1.5, 8.0 / 3.0, -1.5, 0.0, 1.0 / 6.0)
penalty_weight = 4.0
REACH = 3
LANES = 128
TILE = 8
F32 = jnp.float32
MESH = pl.DeviceIdType.MESH


def dot(a, b, a_dim, b_dim, precision=lax.Precision.HIGH):
    return lax.dot_general(
        a,
        b,
        (((a_dim,), (b_dim,)), ((), ())),
        precision=precision,
        preferred_element_type=F32,
    )


exact_dot = functools.partial(dot, precision=lax.Precision.HIGHEST)


def iota(shape, dim):
    return lax.broadcasted_iota(jnp.int32, shape, dim)


def taps_at(offset, taps):
    out = jnp.zeros(offset.shape, F32)
    for o in range(-REACH, REACH + 1):
        if taps[o + REACH] != 0.0:
            out = jnp.where(offset == o, F32(taps[o + REACH]), out)
    return out


def span_sum(ext_ref, taps, rows):
    total = F32(taps[REACH]) * ext_ref[REACH : REACH + rows]
    for o in range(1, REACH + 1):
        if taps[REACH + o] != 0.0:
            pair = ext_ref[REACH - o : REACH - o + rows] + ext_ref[REACH + o : REACH + o + rows]
            total = total + F32(taps[REACH + o]) * pair
    return total


def eliminate(table, first, count):
    row_at = iota(table.shape, 0)
    columns = [
        jnp.broadcast_to(table[:, first + k : first + k + 1], table.shape) for k in range(count)
    ]
    for k in range(count):
        factor = columns[k]
        inverse = 1.0 / factor[k : k + 1, :]

        def reduce(x):
            row = x[k : k + 1, :] * inverse
            return jnp.where(row_at == k, row, x - factor * row)

        table = reduce(table)
        for j in range(k + 1, count):
            columns[j] = reduce(columns[j])
    return table


def kernel(
    n,
    N,
    right_hbm,
    scale_hbm,
    extra_hbm,
    line_hbm,
    partner_hbm,
    solution_ref,
    residual_ref,
    right_ref,
    scale_ref,
    extra_ref,
    line_ref,
    partner_ref,
    basis,
    weighted,
    halo_out,
    halo,
    iface,
    rim,
    corner,
    ext_m,
    ext_b,
    early_c,
    early_s,
    late_c,
    late_s,
    rim_sems,
    halo_sems,
    corner_sems,
    iface_sems,
    chord_sems,
    span_sems,
    load_sems,
):
    C, R, L = right_ref.shape
    RC = R * C
    slots = line_ref.shape[0]
    s = lax.axis_index("span")
    c = lax.axis_index("chord")
    right, left = lax.rem(c + 1, n), lax.rem(c + n - 1, n)
    above, below = s > 0, s < N - 1

    loads = [
        pltpu.make_async_copy(src, dst, load_sems.at[k])
        for k, (src, dst) in enumerate(
            (
                (right_hbm, right_ref),
                (scale_hbm, scale_ref),
                (extra_hbm, extra_ref),
                (line_hbm, line_ref),
                (partner_hbm, partner_ref),
            )
        )
    ]
    for load in loads:
        load.start()

    barrier = pltpu.get_barrier_semaphore()
    for d in range(1, n):
        pl.semaphore_signal(barrier, inc=1, device_id=(s, lax.rem(c + d, n)), device_id_type=MESH)
    for d in range(1, N):
        pl.semaphore_signal(barrier, inc=1, device_id=(lax.rem(s + d, N), c), device_id_type=MESH)

    @pl.when(above)
    def _():
        for side in (left, right):
            pl.semaphore_signal(barrier, inc=1, device_id=(s - 1, side), device_id_type=MESH)

    @pl.when(below)
    def _():
        for side in (left, right):
            pl.semaphore_signal(barrier, inc=1, device_id=(s + 1, side), device_id_type=MESH)

    @pl.when(jnp.logical_not(above))
    def _():
        for t in range(2):
            rim[t, 0] = jnp.zeros(rim.shape[2:], F32)
            corner[t, 0] = jnp.zeros(corner.shape[2:], F32)

    @pl.when(jnp.logical_not(below))
    def _():
        for t in range(2):
            rim[t, 1] = jnp.zeros(rim.shape[2:], F32)
            corner[t, 1] = jnp.zeros(corner.shape[2:], F32)

    offset = iota((L, L), 0) - iota((L, L), 1)
    band = jnp.concatenate([taps_at(offset, mass_taps), taps_at(offset, bend_taps)], axis=1)
    k_at, c_at = iota((2 * TILE, L), 0), iota((2 * TILE, L), 1)
    from_left = jnp.logical_and(k_at >= REACH, k_at < 2 * REACH)
    from_right = jnp.logical_and(k_at >= TILE, k_at < TILE + REACH)
    place = jnp.where(k_at < TILE, k_at - 2 * REACH, L + k_at - TILE)
    reach = jnp.where(jnp.logical_or(from_left, from_right), place - c_at, 2 * L)
    side_band = jnp.concatenate([taps_at(reach, mass_taps), taps_at(reach, bend_taps)], axis=1)
    h_at, hc_at = iota((TILE, L), 0), iota((TILE, L), 1)
    halo_line = jnp.where(h_at < REACH, h_at, L - 2 * REACH + h_at)
    halo_pick = jnp.where(
        jnp.logical_and(h_at < 2 * REACH, halo_line == hc_at), F32(1.0), F32(0.0)
    )

    for load in loads:
        load.wait()

    q_at, qc_at = iota((slots, L), 0), iota((slots, L), 1)
    j_at, jc_at = iota((n * slots, L), 0), iota((n * slots, L), 1)
    pick = jnp.zeros((slots, L), F32)
    spread = jnp.zeros((n * slots, L), F32)
    for q in range(slots):
        line, mate = line_ref[q], partner_ref[q]
        pick = jnp.where(jnp.logical_and(q_at == q, qc_at == line), F32(1.0), pick)
        owner = lax.div(mate, jnp.int32(slots))
        away = c - owner
        away = jnp.where(away < 0, away + n, away)
        at = away * slots + (mate - owner * slots)
        spread = jnp.where(jnp.logical_and(j_at == at, jc_at == line), F32(-penalty_weight), spread)
    on_line = jnp.sum(pick, axis=0, keepdims=True)

    scale = scale_ref[...][:, None, :]
    diag = (extra_ref[...] + F32(penalty_weight) * on_line)[:, None, :]

    basis[0] = jnp.swapaxes(right_ref[...], 0, 1)

    def remote(src, dst, sems, at, to):
        return pltpu.make_async_remote_copy(
            src_ref=src,
            dst_ref=dst,
            send_sem=sems.at[(0,) + at],
            recv_sem=sems.at[(1,) + at],
            device_id=to,
            device_id_type=MESH,
        )

    def flat(t):
        return basis[t].reshape(RC, L)

    def wide(t):
        return jnp.concatenate([basis[t, r] for r in range(R)], axis=1)

    def copies(t):
        down = [remote(weighted.at[t, pl.ds(R - REACH, REACH)], rim.at[t, 0], rim_sems, (t, 0), (s + 1, c))]
        up = [remote(weighted.at[t, pl.ds(0, REACH)], rim.at[t, 1], rim_sems, (t, 1), (s - 1, c))]
        last, first = pl.ds(RC - LANES, LANES), pl.ds(0, LANES)
        for k, to in enumerate((right, left)):
            spot = pl.ds(k * TILE, TILE)
            down.append(
                remote(halo_out.at[t, :, last], corner.at[t, 0, spot], corner_sems, (t, 0, k), (s + 1, to))
            )
            up.append(
                remote(halo_out.at[t, :, first], corner.at[t, 1, spot], corner_sems, (t, 1, k), (s - 1, to))
            )
        around = []
        for k, to in enumerate((right, left)):
            spot = pl.ds(k * TILE, TILE)
            around.append(remote(halo_out.at[t], halo.at[t, spot], halo_sems, (t, k), (s, to)))
        for d in range(1, n):
            around.append(
                remote(
                    iface.at[t, pl.ds(0, slots)],
                    iface.at[t, pl.ds(d * slots, slots)],
                    iface_sems,
                    (t, d),
                    (s, lax.rem(c + d, n)),
                )
            )
        return down, up, around

    def prepare(t):
        w = scale * basis[t]
        weighted[t] = w
        halo_out[t] = dot(halo_pick, w.reshape(RC, L), 1, 1)
        iface[t, 0:slots] = dot(pick, flat(t), 1, 1)

    def send(t):
        down, up, around = copies(t)

        @pl.when(below)
        def _():
            for copy in down:
                copy.start()

        @pl.when(above)
        def _():
            for copy in up:
                copy.start()

        for copy in around:
            copy.start()

    def inner(t):
        both = dot(weighted[t].reshape(RC, L), band, 1, 0)
        ext_m[REACH : REACH + R] = both[:, :L].reshape(R, C, L)
        ext_b[REACH : REACH + R] = both[:, L:].reshape(R, C, L)

    def receive(t):
        down, up, around = copies(t)

        @pl.when(above)
        def _():
            for copy in down:
                copy.wait_recv()

        @pl.when(below)
        def _():
            for copy in up:
                copy.wait_recv()

        for copy in around:
            copy.wait_recv()

    def sent(t):
        down, up, around = copies(t)

        @pl.when(below)
        def _():
            for copy in down:
                copy.wait_send()

        @pl.when(above)
        def _():
            for copy in up:
                copy.wait_send()

        for copy in around:
            copy.wait_send()

    def outer(t):
        edge = REACH * C
        ends = dot(rim[t].reshape(2 * edge, L), band, 1, 0)
        top = ends[:edge] + dot(corner[t, 0], side_band, 0, 0)[LANES - edge :]
        low = ends[edge:] + dot(corner[t, 1], side_band, 0, 0)[:edge]
        mid = dot(halo[t], side_band, 0, 0)
        ext_m[0:REACH] = top[:, :L].reshape(REACH, C, L)
        ext_b[0:REACH] = top[:, L:].reshape(REACH, C, L)
        ext_m[REACH + R :] = low[:, :L].reshape(REACH, C, L)
        ext_b[REACH + R :] = low[:, L:].reshape(REACH, C, L)
        ext_m[REACH : REACH + R] += mid[:, :L].reshape(R, C, L)
        ext_b[REACH : REACH + R] += mid[:, L:].reshape(R, C, L)
        y = span_sum(ext_m, bend_taps, R) + span_sum(ext_b, mass_taps, R)
        coupled = dot(iface[t], spread, 0, 0).reshape(R, C, L)
        basis[t + 1] = scale * y + diag * basis[t] + coupled

    def group_copies(buf, sems, which, count, to):
        return [remote(buf.at[0], buf.at[d], sems, (which, d), to(d)) for d in range(1, count)]

    def along_chord(d):
        return (s, lax.rem(c + d, n))

    def along_span(d):
        return (lax.rem(s + d, N), c)

    def total(buf, count):
        out = buf[0]
        for d in range(1, count):
            out = out + buf[d]
        return out

    def pad(x):
        return jnp.concatenate([x, jnp.zeros((x.shape[0], LANES - x.shape[1]), F32)], axis=1)

    ec = group_copies(early_c, chord_sems, 0, n, along_chord)
    es = group_copies(early_s, span_sems, 0, N, along_span)
    lc = group_copies(late_c, chord_sems, 1, n, along_chord)
    ls = group_copies(late_s, span_sems, 1, N, along_span)

    prepare(0)
    greeted = (n - 1) + (N - 1) + 2 * (above.astype(jnp.int32) + below.astype(jnp.int32))
    pl.semaphore_wait(barrier, greeted)
    send(0)
    inner(0)
    receive(0)
    outer(0)
    prepare(1)
    send(1)

    v0, v1 = wide(0), wide(1)
    first = exact_dot(v0, jnp.concatenate([v1, v0], axis=0), 1, 1)
    g11 = exact_dot(v1, v1, 1, 1)
    early_c[0] = pad(jnp.concatenate([first[:, :C], g11, first[:, C:]], axis=1))
    for copy in ec:
        copy.start()
    inner(1)
    for copy in ec:
        copy.wait_recv()
    early_s[0] = total(early_c, n)
    for copy in es:
        copy.start()
    receive(1)
    outer(1)
    late_c[0] = pad(exact_dot(wide(1), jnp.concatenate([wide(0), wide(2)], axis=0), 1, 1))
    for copy in lc:
        copy.start()
    for copy in es:
        copy.wait_recv()
    table = total(early_s, N)
    g01, g11 = table[:, :C], table[:, C : 2 * C]
    table = eliminate(table, 0, C)
    folded = exact_dot(g11, table, 1, 0)
    slope = table[:, C : 2 * C]
    step = table[:, 2 * C : 3 * C]
    lead = pad(jnp.concatenate([jnp.zeros((C, 2 * C), F32), g01], axis=1))
    rest = lead - folded
    for copy in lc:
        copy.wait_recv()
    late_s[0] = total(late_c, n)
    for copy in ls:
        copy.start()
    for copy in ls:
        copy.wait_recv()
    table = eliminate(rest + total(late_s, N), C, C)
    y1 = table[:, 2 * C : 3 * C]
    y0 = step - exact_dot(slope, y1, 1, 0)
    mix = jnp.concatenate([y0, y1], axis=0)

    v0, v1, v2 = wide(0), wide(1), wide(2)
    found = dot(mix, jnp.concatenate([v0, v1], axis=0), 0, 0)
    left_over = v0 - dot(mix, jnp.concatenate([v1, v2], axis=0), 0, 0)

    def narrow(x):
        rows = jnp.stack([x[:, r * L : (r + 1) * L] for r in range(R)], axis=0)
        return jnp.swapaxes(rows, 0, 1)

    solution_ref[...] = narrow(found)
    residual_ref[...] = narrow(left_over)
    sent(0)
    sent(1)
    for copy in ec + es + lc + ls:
        copy.wait_send()


def body(n, N, right_side, stiff_scale, extra_diag, iface_line, partner):
    C, R, L = right_side.shape
    slots = iface_line.shape[0]
    vmem = pl.BlockSpec(memory_space=pltpu.VMEM)
    hbm = pl.BlockSpec(memory_space=pltpu.HBM)
    dma = pltpu.SemaphoreType.DMA
    field = jax.ShapeDtypeStruct((C, R, L), F32)
    return pl.pallas_call(
        functools.partial(kernel, n, N),
        out_shape=(field, field),
        in_specs=[hbm] * 5,
        out_specs=(vmem, vmem),
        scratch_shapes=[
            pltpu.VMEM((C, R, L), F32),
            pltpu.VMEM((R, L), F32),
            pltpu.VMEM((R, L), F32),
            pltpu.SMEM((slots,), jnp.int32),
            pltpu.SMEM((slots,), jnp.int32),
            pltpu.VMEM((3, R, C, L), F32),
            pltpu.VMEM((2, R, C, L), F32),
            pltpu.VMEM((2, TILE, R * C), F32),
            pltpu.VMEM((2, 2 * TILE, R * C), F32),
            pltpu.VMEM((2, n * slots, R * C), F32),
            pltpu.VMEM((2, 2, REACH, C, L), F32),
            pltpu.VMEM((2, 2, 2 * TILE, LANES), F32),
            pltpu.VMEM((R + 2 * REACH, C, L), F32),
            pltpu.VMEM((R + 2 * REACH, C, L), F32),
            pltpu.VMEM((n, C, LANES), F32),
            pltpu.VMEM((N, C, LANES), F32),
            pltpu.VMEM((n, C, LANES), F32),
            pltpu.VMEM((N, C, LANES), F32),
            dma((2, 2, 2)),
            dma((2, 2, 2)),
            dma((2, 2, 2, 2)),
            dma((2, 2, n)),
            dma((2, 2, n)),
            dma((2, 2, N)),
            dma((5,)),
        ],
        compiler_params=pltpu.CompilerParams(
            collective_id=0, has_side_effects=True, vmem_limit_bytes=64 * 1024 * 1024
        ),
        name="shell_cg",
    )(right_side, stiff_scale, extra_diag, iface_line, partner)


def solution(mesh):
    sizes = dict(mesh.shape)
    return jax.shard_map(
        functools.partial(body, sizes["chord"], sizes["span"]),
        mesh=mesh,
        in_specs=(
            P(None, "span", "chord"),
            P("span", "chord"),
            P("span", "chord"),
            P("chord"),
            P("chord"),
        ),
        out_specs=(P(None, "span", "chord"), P(None, "span", "chord")),
        check_vma=False,
    )
```

```python
import functools

import jax
import jax.numpy as jnp
from jax import lax
from jax.experimental import pallas as pl
from jax.experimental.pallas import tpu as pltpu
from jax.sharding import PartitionSpec as P

mass_taps = (1.0, 120.0, 1191.0, 2416.0, 1191.0, 120.0, 1.0)
mass_high = (1.0, 120.0, 1192.0, 2416.0, 1192.0, 120.0, 1.0)
mass_low = (0.0, 0.0, -1.0, 0.0, -1.0, 0.0, 0.0)
bend_taps = (1.0, 0.0, -9.0, 16.0, -9.0, 0.0, 1.0)
tap_unit = 1.0 / (5040.0 * 6.0)
penalty_weight = 4.0
REACH = 3
LANES = 128
TILE = 8
F32 = jnp.float32
MESH = pl.DeviceIdType.MESH


def dot(a, b, a_dim, b_dim, precision=lax.Precision.HIGH):
    return lax.dot_general(
        a,
        b,
        (((a_dim,), (b_dim,)), ((), ())),
        precision=precision,
        preferred_element_type=F32,
    )


def product(a, b, a_dim, b_dim):
    return lax.dot_general(a, b, (((a_dim,), (b_dim,)), ((), ())), preferred_element_type=F32)


def split(x):
    high = x.astype(jnp.bfloat16)
    rest = x - high.astype(F32)
    mid = rest.astype(jnp.bfloat16)
    low = (rest - mid.astype(F32)).astype(jnp.bfloat16)
    return high, mid, low


exact_dot = functools.partial(dot, precision=lax.Precision.HIGHEST)


def iota(shape, dim):
    return lax.broadcasted_iota(jnp.int32, shape, dim)


def taps_at(offset, taps):
    out = jnp.zeros(offset.shape, F32)
    for o in range(-REACH, REACH + 1):
        if taps[o + REACH] != 0.0:
            out = jnp.where(offset == o, F32(taps[o + REACH]), out)
    return out


def span_sum(ext_ref, taps, rows):
    total = F32(taps[REACH]) * ext_ref[REACH : REACH + rows]
    for o in range(1, REACH + 1):
        if taps[REACH + o] != 0.0:
            pair = ext_ref[REACH - o : REACH - o + rows] + ext_ref[REACH + o : REACH + o + rows]
            total = total + F32(taps[REACH + o]) * pair
    return total


def eliminate(table, first, count):
    row_at = iota(table.shape, 0)
    columns = [
        jnp.broadcast_to(table[:, first + k : first + k + 1], table.shape) for k in range(count)
    ]
    for k in range(count):
        factor = columns[k]
        inverse = 1.0 / factor[k : k + 1, :]

        def reduce(x):
            row = x[k : k + 1, :] * inverse
            return jnp.where(row_at == k, row, x - factor * row)

        table = reduce(table)
        for j in range(k + 1, count):
            columns[j] = reduce(columns[j])
    return table


def kernel(
    n,
    N,
    right_hbm,
    scale_hbm,
    extra_hbm,
    line_hbm,
    partner_hbm,
    solution_ref,
    residual_ref,
    right_ref,
    scale_ref,
    extra_ref,
    line_ref,
    partner_ref,
    basis,
    weighted,
    terms,
    w_terms,
    halo_out,
    halo,
    iface,
    rim,
    corner,
    ext_m,
    ext_b,
    early_c,
    early_s,
    late_c,
    late_s,
    rim_sems,
    halo_sems,
    corner_sems,
    iface_sems,
    chord_sems,
    span_sems,
    load_sems,
):
    C, R, L = right_ref.shape
    RC = R * C
    slots = line_ref.shape[0]
    s = lax.axis_index("span")
    c = lax.axis_index("chord")
    right, left = lax.rem(c + 1, n), lax.rem(c + n - 1, n)
    above, below = s > 0, s < N - 1

    loads = [
        pltpu.make_async_copy(src, dst, load_sems.at[k])
        for k, (src, dst) in enumerate(
            (
                (right_hbm, right_ref),
                (scale_hbm, scale_ref),
                (extra_hbm, extra_ref),
                (line_hbm, line_ref),
                (partner_hbm, partner_ref),
            )
        )
    ]
    for load in loads:
        load.start()

    barrier = pltpu.get_barrier_semaphore()
    for d in range(1, n):
        pl.semaphore_signal(barrier, inc=1, device_id=(s, lax.rem(c + d, n)), device_id_type=MESH)
    for d in range(1, N):
        pl.semaphore_signal(barrier, inc=1, device_id=(lax.rem(s + d, N), c), device_id_type=MESH)

    @pl.when(above)
    def _():
        for side in (left, right):
            pl.semaphore_signal(barrier, inc=1, device_id=(s - 1, side), device_id_type=MESH)

    @pl.when(below)
    def _():
        for side in (left, right):
            pl.semaphore_signal(barrier, inc=1, device_id=(s + 1, side), device_id_type=MESH)

    @pl.when(jnp.logical_not(above))
    def _():
        for t in range(2):
            rim[t, 0] = jnp.zeros(rim.shape[2:], F32)
            corner[t, 0] = jnp.zeros(corner.shape[2:], F32)

    @pl.when(jnp.logical_not(below))
    def _():
        for t in range(2):
            rim[t, 1] = jnp.zeros(rim.shape[2:], F32)
            corner[t, 1] = jnp.zeros(corner.shape[2:], F32)

    offset = iota((L, L), 0) - iota((L, L), 1)

    def bands(at):
        bend = taps_at(at, bend_taps)
        high = jnp.concatenate([taps_at(at, mass_high), bend], axis=1)
        low = jnp.concatenate([taps_at(at, mass_low), jnp.zeros_like(bend)], axis=1)
        return jnp.concatenate([high, high, high, low], axis=0).astype(jnp.bfloat16)

    band = bands(offset)
    k_at, c_at = iota((2 * TILE, L), 0), iota((2 * TILE, L), 1)
    from_left = jnp.logical_and(k_at >= REACH, k_at < 2 * REACH)
    from_right = jnp.logical_and(k_at >= TILE, k_at < TILE + REACH)
    place = jnp.where(k_at < TILE, k_at - 2 * REACH, L + k_at - TILE)
    reach = jnp.where(jnp.logical_or(from_left, from_right), place - c_at, 2 * L)
    side_band = bands(reach)
    h_at, hc_at = iota((2 * TILE, L), 0), iota((2 * TILE, L), 1)
    halo_line = jnp.where(h_at < REACH, h_at, L - 2 * REACH + h_at)
    halo_pick = jnp.where(
        jnp.logical_and(h_at < 2 * REACH, halo_line == hc_at), F32(1.0), F32(0.0)
    )

    for load in loads:
        load.wait()

    halo_pick = jnp.concatenate([halo_pick] * 3, axis=1).astype(jnp.bfloat16)

    q_at, qc_at = iota((2 * TILE, L), 0), iota((2 * TILE, L), 1)
    j_at, jc_at = iota((n * slots, L), 0), iota((n * slots, L), 1)
    pick = jnp.zeros((2 * TILE, L), F32)
    spread = jnp.zeros((n * slots, L), F32)
    for q in range(slots):
        line, mate = line_ref[q], partner_ref[q]
        pick = jnp.where(jnp.logical_and(q_at == q, qc_at == line), F32(1.0), pick)
        owner = lax.div(mate, jnp.int32(slots))
        away = c - owner
        away = jnp.where(away < 0, away + n, away)
        at = away * slots + (mate - owner * slots)
        spread = jnp.where(jnp.logical_and(j_at == at, jc_at == line), F32(-penalty_weight), spread)
    on_line = jnp.sum(pick, axis=0, keepdims=True)
    pick = jnp.concatenate([pick] * 3, axis=1).astype(jnp.bfloat16)
    spread = jnp.concatenate([spread] * 3, axis=0).astype(jnp.bfloat16)

    scale = scale_ref[...][:, None, :]
    diag = (extra_ref[...] + F32(penalty_weight) * on_line)[:, None, :]

    def remote(src, dst, sems, at, to):
        return pltpu.make_async_remote_copy(
            src_ref=src,
            dst_ref=dst,
            send_sem=sems.at[(0,) + at],
            recv_sem=sems.at[(1,) + at],
            device_id=to,
            device_id_type=MESH,
        )

    def keep(t, field):
        basis[t] = field
        for k, term in enumerate(split(field)):
            terms[t, :, k * C : (k + 1) * C] = term

    def wide(t, count=3):
        return jnp.concatenate([terms[t, r, 0 : count * C] for r in range(R)], axis=1)

    def stacked(x, axis):
        high, mid, low = split(x)
        return jnp.concatenate([high, mid, low, high], axis=axis)

    def copies(t):
        down = [remote(weighted.at[t, pl.ds(R - REACH, REACH)], rim.at[t, 0], rim_sems, (t, 0), (s + 1, c))]
        up = [remote(weighted.at[t, pl.ds(0, REACH)], rim.at[t, 1], rim_sems, (t, 1), (s - 1, c))]
        last, first = pl.ds(RC - LANES, LANES), pl.ds(0, LANES)
        for k, to in enumerate((right, left)):
            spot = pl.ds(k * TILE, TILE)
            down.append(
                remote(halo_out.at[t, :, last], corner.at[t, 0, spot], corner_sems, (t, 0, k), (s + 1, to))
            )
            up.append(
                remote(halo_out.at[t, :, first], corner.at[t, 1, spot], corner_sems, (t, 1, k), (s - 1, to))
            )
        around = []
        for k, to in enumerate((right, left)):
            spot = pl.ds(k * TILE, TILE)
            around.append(remote(halo_out.at[t], halo.at[t, spot], halo_sems, (t, k), (s, to)))
        for d in range(1, n):
            around.append(
                remote(
                    iface.at[t, pl.ds(0, slots)],
                    iface.at[t, pl.ds(d * slots, slots)],
                    iface_sems,
                    (t, d),
                    (s, lax.rem(c + d, n)),
                )
            )
        return down, up, around

    def prepare(t):
        w = scale * basis[t]
        weighted[t] = w
        w_terms[...] = stacked(w.reshape(RC, L), 1)
        halo_out[t] = product(halo_pick, w_terms[:, 0 : 3 * L], 1, 1)[:TILE]
        v = jnp.concatenate(
            [terms[t, :, k * C : (k + 1) * C].reshape(RC, L) for k in range(3)], axis=1
        )
        iface[t, 0:slots] = product(pick, v, 1, 1)[:slots]

    def send(t):
        down, up, around = copies(t)

        @pl.when(below)
        def _():
            for copy in down:
                copy.start()

        @pl.when(above)
        def _():
            for copy in up:
                copy.start()

        for copy in around:
            copy.start()

    def inner():
        both = product(w_terms[...], band, 1, 0)
        ext_m[REACH : REACH + R] = both[:, :L].reshape(R, C, L)
        ext_b[REACH : REACH + R] = both[:, L:].reshape(R, C, L)

    def receive(t):
        down, up, around = copies(t)

        @pl.when(above)
        def _():
            for copy in down:
                copy.wait_recv()

        @pl.when(below)
        def _():
            for copy in up:
                copy.wait_recv()

        for copy in around:
            copy.wait_recv()

    def sent(t):
        down, up, around = copies(t)

        @pl.when(below)
        def _():
            for copy in down:
                copy.wait_send()

        @pl.when(above)
        def _():
            for copy in up:
                copy.wait_send()

        for copy in around:
            copy.wait_send()

    def outer(t):
        edge = REACH * C
        ends = product(stacked(rim[t].reshape(2 * edge, L), 1), band, 1, 0)
        top = ends[:edge] + product(stacked(corner[t, 0], 0), side_band, 0, 0)[LANES - edge :]
        low = ends[edge:] + product(stacked(corner[t, 1], 0), side_band, 0, 0)[:edge]
        mid = product(stacked(halo[t], 0), side_band, 0, 0)
        ext_m[0:REACH] = top[:, :L].reshape(REACH, C, L)
        ext_b[0:REACH] = top[:, L:].reshape(REACH, C, L)
        ext_m[REACH + R :] = low[:, :L].reshape(REACH, C, L)
        ext_b[REACH + R :] = low[:, L:].reshape(REACH, C, L)
        ext_m[REACH : REACH + R] += mid[:, :L].reshape(R, C, L)
        ext_b[REACH : REACH + R] += mid[:, L:].reshape(R, C, L)
        y = span_sum(ext_m, bend_taps, R) + span_sum(ext_b, mass_taps, R)
        lines = jnp.concatenate(split(iface[t]), axis=0)
        coupled = product(lines, spread, 0, 0).reshape(R, C, L)
        keep(t + 1, (scale * F32(tap_unit)) * y + diag * basis[t] + coupled)

    def group_copies(buf, sems, which, count, to):
        return [remote(buf.at[0], buf.at[d], sems, (which, d), to(d)) for d in range(1, count)]

    def along_chord(d):
        return (s, lax.rem(c + d, n))

    def along_span(d):
        return (lax.rem(s + d, N), c)

    def total(buf, count):
        out = buf[0]
        for d in range(1, count):
            out = out + buf[d]
        return out

    def pad(x):
        return jnp.concatenate([x, jnp.zeros((x.shape[0], LANES - x.shape[1]), F32)], axis=1)

    ec = group_copies(early_c, chord_sems, 0, n, along_chord)
    es = group_copies(early_s, span_sems, 0, N, along_span)
    lc = group_copies(late_c, chord_sems, 1, n, along_chord)
    ls = group_copies(late_s, span_sems, 1, N, along_span)

    def gram(table, i, j):
        block = table[3 * C * i : 3 * C * (i + 1), 3 * C * j : 3 * C * (j + 1)]
        rows = block[:C] + block[C : 2 * C] + block[2 * C :]
        return rows[:, :C] + rows[:, C : 2 * C] + rows[:, 2 * C :]

    keep(0, jnp.swapaxes(right_ref[...], 0, 1))
    prepare(0)
    greeted = (n - 1) + (N - 1) + 2 * (above.astype(jnp.int32) + below.astype(jnp.int32))
    pl.semaphore_wait(barrier, greeted)
    send(0)
    inner()
    receive(0)
    outer(0)
    prepare(1)
    send(1)

    pair = jnp.concatenate([wide(0), wide(1)], axis=0)
    early = product(pair, pair, 1, 1)
    early_c[0] = pad(
        jnp.concatenate([gram(early, 0, 1), gram(early, 1, 1), gram(early, 0, 0)], axis=1)
    )
    for copy in ec:
        copy.start()
    inner()
    for copy in ec:
        copy.wait_recv()
    early_s[0] = total(early_c, n)
    for copy in es:
        copy.start()
    receive(1)
    outer(1)
    late = gram(product(wide(1), wide(2), 1, 1), 0, 0)
    late_c[0] = pad(jnp.concatenate([jnp.zeros((C, C), F32), late], axis=1))
    for copy in lc:
        copy.start()
    for copy in es:
        copy.wait_recv()
    table = total(early_s, N)
    g01, g11 = table[:, :C], table[:, C : 2 * C]
    table = eliminate(table, 0, C)
    folded = exact_dot(g11, table, 1, 0)
    slope = table[:, C : 2 * C]
    step = table[:, 2 * C : 3 * C]
    lead = pad(jnp.concatenate([jnp.zeros((C, 2 * C), F32), g01], axis=1))
    rest = lead - folded
    for copy in lc:
        copy.wait_recv()
    late_s[0] = total(late_c, n)
    for copy in ls:
        copy.start()
    for copy in ls:
        copy.wait_recv()
    table = eliminate(rest + total(late_s, N), C, C)
    y1 = table[:, 2 * C : 3 * C]
    y0 = step - exact_dot(slope, y1, 1, 0)
    (a0, b0, c0), (a1, b1, c1) = split(y0), split(y1)
    mix = jnp.concatenate([a0, a0, a0, a1, a1, a1, b0, b0, b1, b1, c0, c1], axis=0)

    def mixed(i, j):
        field = jnp.concatenate(
            [wide(i), wide(j), wide(i, 2), wide(j, 2), wide(i, 1), wide(j, 1)], axis=0
        )
        return product(mix, field, 0, 0)

    found = mixed(0, 1)
    start = jnp.concatenate([basis[0, r] for r in range(R)], axis=1)
    left_over = start - mixed(1, 2)

    def narrow(x):
        rows = jnp.stack([x[:, r * L : (r + 1) * L] for r in range(R)], axis=0)
        return jnp.swapaxes(rows, 0, 1)

    solution_ref[...] = narrow(found)
    residual_ref[...] = narrow(left_over)
    sent(0)
    sent(1)
    for copy in ec + es + lc + ls:
        copy.wait_send()


def body(n, N, right_side, stiff_scale, extra_diag, iface_line, partner):
    C, R, L = right_side.shape
    slots = iface_line.shape[0]
    vmem = pl.BlockSpec(memory_space=pltpu.VMEM)
    hbm = pl.BlockSpec(memory_space=pltpu.HBM)
    dma = pltpu.SemaphoreType.DMA
    field = jax.ShapeDtypeStruct((C, R, L), F32)
    return pl.pallas_call(
        functools.partial(kernel, n, N),
        out_shape=(field, field),
        in_specs=[hbm] * 5,
        out_specs=(vmem, vmem),
        scratch_shapes=[
            pltpu.VMEM((C, R, L), F32),
            pltpu.VMEM((R, L), F32),
            pltpu.VMEM((R, L), F32),
            pltpu.SMEM((slots,), jnp.int32),
            pltpu.SMEM((slots,), jnp.int32),
            pltpu.VMEM((3, R, C, L), F32),
            pltpu.VMEM((2, R, C, L), F32),
            pltpu.VMEM((3, R, 3 * C, L), jnp.bfloat16),
            pltpu.VMEM((R * C, 4 * L), jnp.bfloat16),
            pltpu.VMEM((2, TILE, R * C), F32),
            pltpu.VMEM((2, 2 * TILE, R * C), F32),
            pltpu.VMEM((2, n * slots, R * C), F32),
            pltpu.VMEM((2, 2, REACH, C, L), F32),
            pltpu.VMEM((2, 2, 2 * TILE, LANES), F32),
            pltpu.VMEM((R + 2 * REACH, C, L), F32),
            pltpu.VMEM((R + 2 * REACH, C, L), F32),
            pltpu.VMEM((n, C, LANES), F32),
            pltpu.VMEM((N, C, LANES), F32),
            pltpu.VMEM((n, C, LANES), F32),
            pltpu.VMEM((N, C, LANES), F32),
            dma((2, 2, 2)),
            dma((2, 2, 2)),
            dma((2, 2, 2, 2)),
            dma((2, 2, n)),
            dma((2, 2, n)),
            dma((2, 2, N)),
            dma((5,)),
        ],
        compiler_params=pltpu.CompilerParams(
            collective_id=0, has_side_effects=True, vmem_limit_bytes=64 * 1024 * 1024 - 2 * 4 * C * R * L
        ),
        name="shell_cg",
    )(right_side, stiff_scale, extra_diag, iface_line, partner)


def solution(mesh):
    sizes = dict(mesh.shape)
    return jax.shard_map(
        functools.partial(body, sizes["chord"], sizes["span"]),
        mesh=mesh,
        in_specs=(
            P(None, "span", "chord"),
            P("span", "chord"),
            P("span", "chord"),
            P("chord"),
            P("chord"),
        ),
        out_specs=(P(None, "span", "chord"), P(None, "span", "chord")),
        check_vma=False,
    )
```

```python
import functools

import jax
import jax.numpy as jnp
from jax import lax
from jax.experimental import pallas as pl
from jax.experimental.pallas import tpu as pltpu
from jax.sharding import PartitionSpec as P

mass_taps = (1.0, 120.0, 1191.0, 2416.0, 1191.0, 120.0, 1.0)
mass_high = (1.0, 120.0, 1192.0, 2416.0, 1192.0, 120.0, 1.0)
mass_low = (0.0, 0.0, -1.0, 0.0, -1.0, 0.0, 0.0)
bend_taps = (1.0, 0.0, -9.0, 16.0, -9.0, 0.0, 1.0)
tap_unit = 1.0 / (5040.0 * 6.0)
penalty_weight = 4.0
REACH = 3
LANES = 128
TILE = 8
F32 = jnp.float32
MESH = pl.DeviceIdType.MESH


def dot(a, b, a_dim, b_dim, precision=lax.Precision.HIGH):
    return lax.dot_general(
        a,
        b,
        (((a_dim,), (b_dim,)), ((), ())),
        precision=precision,
        preferred_element_type=F32,
    )


def product(a, b, a_dim, b_dim):
    return lax.dot_general(a, b, (((a_dim,), (b_dim,)), ((), ())), preferred_element_type=F32)


def split(x):
    high = x.astype(jnp.bfloat16)
    rest = x - high.astype(F32)
    mid = rest.astype(jnp.bfloat16)
    low = (rest - mid.astype(F32)).astype(jnp.bfloat16)
    return high, mid, low


exact_dot = functools.partial(dot, precision=lax.Precision.HIGHEST)


def iota(shape, dim):
    return lax.broadcasted_iota(jnp.int32, shape, dim)


def taps_at(offset, taps):
    out = jnp.zeros(offset.shape, F32)
    for o in range(-REACH, REACH + 1):
        if taps[o + REACH] != 0.0:
            out = jnp.where(offset == o, F32(taps[o + REACH]), out)
    return out


def span_sum(ext_ref, taps, rows):
    total = F32(taps[REACH]) * ext_ref[REACH : REACH + rows]
    for o in range(1, REACH + 1):
        if taps[REACH + o] != 0.0:
            pair = ext_ref[REACH - o : REACH - o + rows] + ext_ref[REACH + o : REACH + o + rows]
            total = total + F32(taps[REACH + o]) * pair
    return total


def eliminate(table, first, count):
    row_at = iota(table.shape, 0)
    columns = [
        jnp.broadcast_to(table[:, first + k : first + k + 1], table.shape) for k in range(count)
    ]
    for k in range(count):
        factor = columns[k]
        inverse = 1.0 / factor[k : k + 1, :]

        def reduce(x):
            row = x[k : k + 1, :] * inverse
            return jnp.where(row_at == k, row, x - factor * row)

        table = reduce(table)
        for j in range(k + 1, count):
            columns[j] = reduce(columns[j])
    return table


def kernel(
    n,
    N,
    right_hbm,
    scale_hbm,
    extra_hbm,
    line_hbm,
    partner_hbm,
    solution_ref,
    residual_ref,
    right_ref,
    scale_ref,
    extra_ref,
    line_ref,
    partner_ref,
    basis,
    weighted,
    terms,
    w_terms,
    halo_out,
    halo,
    iface,
    rim,
    corner,
    ext_m,
    ext_b,
    early_c,
    early_s,
    late_c,
    late_s,
    rim_sems,
    halo_sems,
    corner_sems,
    iface_sems,
    chord_sems,
    span_sems,
    load_sems,
):
    C, R, L = right_ref.shape
    RC = R * C
    slots = line_ref.shape[0]
    s = lax.axis_index("span")
    c = lax.axis_index("chord")
    right, left = lax.rem(c + 1, n), lax.rem(c + n - 1, n)
    above, below = s > 0, s < N - 1

    loads = [
        pltpu.make_async_copy(src, dst, load_sems.at[k])
        for k, (src, dst) in enumerate(
            (
                (right_hbm, right_ref),
                (scale_hbm, scale_ref),
                (extra_hbm, extra_ref),
                (line_hbm, line_ref),
                (partner_hbm, partner_ref),
            )
        )
    ]
    for load in loads:
        load.start()

    barrier = pltpu.get_barrier_semaphore()
    for d in range(1, n):
        pl.semaphore_signal(barrier, inc=1, device_id=(s, lax.rem(c + d, n)), device_id_type=MESH)
    for d in range(1, N):
        pl.semaphore_signal(barrier, inc=1, device_id=(lax.rem(s + d, N), c), device_id_type=MESH)

    @pl.when(above)
    def _():
        for side in (left, right):
            pl.semaphore_signal(barrier, inc=1, device_id=(s - 1, side), device_id_type=MESH)

    @pl.when(below)
    def _():
        for side in (left, right):
            pl.semaphore_signal(barrier, inc=1, device_id=(s + 1, side), device_id_type=MESH)

    @pl.when(jnp.logical_not(above))
    def _():
        for t in range(2):
            rim[t, 0] = jnp.zeros(rim.shape[2:], F32)
            corner[t, 0] = jnp.zeros(corner.shape[2:], F32)

    @pl.when(jnp.logical_not(below))
    def _():
        for t in range(2):
            rim[t, 1] = jnp.zeros(rim.shape[2:], F32)
            corner[t, 1] = jnp.zeros(corner.shape[2:], F32)

    offset = iota((L, L), 0) - iota((L, L), 1)

    def bands(at):
        bend = taps_at(at, bend_taps)
        high = jnp.concatenate([taps_at(at, mass_high), bend], axis=1)
        low = jnp.concatenate([taps_at(at, mass_low), jnp.zeros_like(bend)], axis=1)
        return jnp.concatenate([high, high, high, low], axis=0).astype(jnp.bfloat16)

    band = bands(offset)
    k_at, c_at = iota((2 * TILE, L), 0), iota((2 * TILE, L), 1)
    from_left = jnp.logical_and(k_at >= REACH, k_at < 2 * REACH)
    from_right = jnp.logical_and(k_at >= TILE, k_at < TILE + REACH)
    place = jnp.where(k_at < TILE, k_at - 2 * REACH, L + k_at - TILE)
    reach = jnp.where(jnp.logical_or(from_left, from_right), place - c_at, 2 * L)
    side_band = bands(reach)
    h_at, hc_at = iota((2 * TILE, L), 0), iota((2 * TILE, L), 1)
    halo_line = jnp.where(h_at < REACH, h_at, L - 2 * REACH + h_at)
    halo_pick = jnp.where(
        jnp.logical_and(h_at < 2 * REACH, halo_line == hc_at), F32(1.0), F32(0.0)
    )

    for load in loads:
        load.wait()

    halo_pick = jnp.concatenate([halo_pick] * 3, axis=1).astype(jnp.bfloat16)

    q_at, qc_at = iota((2 * TILE, L), 0), iota((2 * TILE, L), 1)
    j_at, jc_at = iota((n * slots, L), 0), iota((n * slots, L), 1)
    pick = jnp.zeros((2 * TILE, L), F32)
    spread = jnp.zeros((n * slots, L), F32)
    for q in range(slots):
        line, mate = line_ref[q], partner_ref[q]
        pick = jnp.where(jnp.logical_and(q_at == q, qc_at == line), F32(1.0), pick)
        owner = lax.div(mate, jnp.int32(slots))
        away = c - owner
        away = jnp.where(away < 0, away + n, away)
        at = away * slots + (mate - owner * slots)
        spread = jnp.where(jnp.logical_and(j_at == at, jc_at == line), F32(-penalty_weight), spread)
    on_line = jnp.sum(pick, axis=0, keepdims=True)
    pick = jnp.concatenate([pick] * 3, axis=1).astype(jnp.bfloat16)
    spread = jnp.concatenate([spread] * 3, axis=0).astype(jnp.bfloat16)

    scale = scale_ref[...][:, None, :]
    diag = (extra_ref[...] + F32(penalty_weight) * on_line)[:, None, :]

    def remote(src, dst, sems, at, to):
        return pltpu.make_async_remote_copy(
            src_ref=src,
            dst_ref=dst,
            send_sem=sems.at[(0,) + at],
            recv_sem=sems.at[(1,) + at],
            device_id=to,
            device_id_type=MESH,
        )

    def keep(t, field):
        basis[t] = field
        for k, term in enumerate(split(field)):
            terms[t, :, k * C : (k + 1) * C] = term

    def wide(t, count=3):
        return jnp.concatenate([terms[t, r, 0 : count * C] for r in range(R)], axis=1)

    def stacked(x, axis):
        high, mid, low = split(x)
        return jnp.concatenate([high, mid, low, high], axis=axis)

    def copies(t):
        down = [remote(weighted.at[t, pl.ds(R - REACH, REACH)], rim.at[t, 0], rim_sems, (t, 0), (s + 1, c))]
        up = [remote(weighted.at[t, pl.ds(0, REACH)], rim.at[t, 1], rim_sems, (t, 1), (s - 1, c))]
        last, first = pl.ds(RC - LANES, LANES), pl.ds(0, LANES)
        for k, to in enumerate((right, left)):
            spot = pl.ds(k * TILE, TILE)
            down.append(
                remote(halo_out.at[t, :, last], corner.at[t, 0, spot], corner_sems, (t, 0, k), (s + 1, to))
            )
            up.append(
                remote(halo_out.at[t, :, first], corner.at[t, 1, spot], corner_sems, (t, 1, k), (s - 1, to))
            )
        around = []
        for k, to in enumerate((right, left)):
            spot = pl.ds(k * TILE, TILE)
            around.append(remote(halo_out.at[t], halo.at[t, spot], halo_sems, (t, k), (s, to)))
        for d in range(1, n):
            around.append(
                remote(
                    iface.at[t, pl.ds(0, slots)],
                    iface.at[t, pl.ds(d * slots, slots)],
                    iface_sems,
                    (t, d),
                    (s, lax.rem(c + d, n)),
                )
            )
        return down, up, around

    def prepare(t):
        w = scale * basis[t]
        weighted[t] = w
        w_terms[...] = stacked(w.reshape(RC, L), 1)
        halo_out[t] = product(halo_pick, w_terms[:, 0 : 3 * L], 1, 1)[:TILE]
        v = jnp.concatenate(
            [terms[t, :, k * C : (k + 1) * C].reshape(RC, L) for k in range(3)], axis=1
        )
        iface[t, 0:slots] = product(pick, v, 1, 1)[:slots]

    def send(t):
        down, up, around = copies(t)

        @pl.when(below)
        def _():
            for copy in down:
                copy.start()

        @pl.when(above)
        def _():
            for copy in up:
                copy.start()

        for copy in around:
            copy.start()

    def inner():
        both = product(w_terms[...], band, 1, 0)
        ext_m[REACH : REACH + R] = both[:, :L].reshape(R, C, L)
        ext_b[REACH : REACH + R] = both[:, L:].reshape(R, C, L)

    def receive(t):
        down, up, around = copies(t)

        @pl.when(above)
        def _():
            for copy in down:
                copy.wait_recv()

        @pl.when(below)
        def _():
            for copy in up:
                copy.wait_recv()

        for copy in around:
            copy.wait_recv()

    def sent(t):
        down, up, around = copies(t)

        @pl.when(below)
        def _():
            for copy in down:
                copy.wait_send()

        @pl.when(above)
        def _():
            for copy in up:
                copy.wait_send()

        for copy in around:
            copy.wait_send()

    def outer(t):
        edge = REACH * C
        ends = product(stacked(rim[t].reshape(2 * edge, L), 1), band, 1, 0)
        top = ends[:edge] + product(stacked(corner[t, 0], 0), side_band, 0, 0)[LANES - edge :]
        low = ends[edge:] + product(stacked(corner[t, 1], 0), side_band, 0, 0)[:edge]
        mid = product(stacked(halo[t], 0), side_band, 0, 0)
        ext_m[0:REACH] = top[:, :L].reshape(REACH, C, L)
        ext_b[0:REACH] = top[:, L:].reshape(REACH, C, L)
        ext_m[REACH + R :] = low[:, :L].reshape(REACH, C, L)
        ext_b[REACH + R :] = low[:, L:].reshape(REACH, C, L)
        ext_m[REACH : REACH + R] += mid[:, :L].reshape(R, C, L)
        ext_b[REACH : REACH + R] += mid[:, L:].reshape(R, C, L)
        y = span_sum(ext_m, bend_taps, R) + span_sum(ext_b, mass_taps, R)
        lines = jnp.concatenate(split(iface[t]), axis=0)
        coupled = product(lines, spread, 0, 0).reshape(R, C, L)
        keep(t + 1, (scale * F32(tap_unit)) * y + diag * basis[t] + coupled)

    def group_copies(buf, sems, which, count, to):
        return [remote(buf.at[0], buf.at[d], sems, (which, d), to(d)) for d in range(1, count)]

    def along_chord(d):
        return (s, lax.rem(c + d, n))

    def along_span(d):
        return (lax.rem(s + d, N), c)

    def total(buf, count):
        out = buf[0]
        for d in range(1, count):
            out = out + buf[d]
        return out

    def pad(x):
        return jnp.concatenate([x, jnp.zeros((x.shape[0], LANES - x.shape[1]), F32)], axis=1)

    ec = group_copies(early_c, chord_sems, 0, n, along_chord)
    es = group_copies(early_s, span_sems, 0, N, along_span)
    lc = group_copies(late_c, chord_sems, 1, n, along_chord)
    ls = group_copies(late_s, span_sems, 1, N, along_span)

    def gram(table, i, j):
        block = table[3 * C * i : 3 * C * (i + 1), 3 * C * j : 3 * C * (j + 1)]
        rows = block[:C] + block[C : 2 * C] + block[2 * C :]
        return rows[:, :C] + rows[:, C : 2 * C] + rows[:, 2 * C :]

    keep(0, jnp.swapaxes(right_ref[...], 0, 1))
    greeted = (n - 1) + (N - 1) + 2 * (above.astype(jnp.int32) + below.astype(jnp.int32))

    @pl.loop(0, 2)
    def _(t):
        prepare(t)

        @pl.when(t == 0)
        def _():
            pl.semaphore_wait(barrier, greeted)

        send(t)

        @pl.when(t == 1)
        def _():
            pair = jnp.concatenate([wide(0), wide(1)], axis=0)
            early = product(pair, pair, 1, 1)
            early_c[0] = pad(
                jnp.concatenate([gram(early, 0, 1), gram(early, 1, 1), gram(early, 0, 0)], axis=1)
            )
            for copy in ec:
                copy.start()

        inner()

        @pl.when(t == 1)
        def _():
            for copy in ec:
                copy.wait_recv()
            early_s[0] = total(early_c, n)
            for copy in es:
                copy.start()

        receive(t)
        outer(t)

    late = gram(product(wide(1), wide(2), 1, 1), 0, 0)
    late_c[0] = pad(jnp.concatenate([jnp.zeros((C, C), F32), late], axis=1))
    for copy in lc:
        copy.start()
    for copy in es:
        copy.wait_recv()
    table = total(early_s, N)
    g01, g11 = table[:, :C], table[:, C : 2 * C]
    table = eliminate(table, 0, C)
    folded = exact_dot(g11, table, 1, 0)
    slope = table[:, C : 2 * C]
    step = table[:, 2 * C : 3 * C]
    lead = pad(jnp.concatenate([jnp.zeros((C, 2 * C), F32), g01], axis=1))
    rest = lead - folded
    for copy in lc:
        copy.wait_recv()
    late_s[0] = total(late_c, n)
    for copy in ls:
        copy.start()
    for copy in ls:
        copy.wait_recv()
    table = eliminate(rest + total(late_s, N), C, C)
    y1 = table[:, 2 * C : 3 * C]
    y0 = step - exact_dot(slope, y1, 1, 0)
    (a0, b0, c0), (a1, b1, c1) = split(y0), split(y1)
    mix = jnp.concatenate([a0, a0, a0, a1, a1, a1, b0, b0, b1, b1, c0, c1], axis=0)

    def mixed(i, j):
        field = jnp.concatenate(
            [wide(i), wide(j), wide(i, 2), wide(j, 2), wide(i, 1), wide(j, 1)], axis=0
        )
        return product(mix, field, 0, 0)

    found = mixed(0, 1)
    start = jnp.concatenate([basis[0, r] for r in range(R)], axis=1)
    left_over = start - mixed(1, 2)

    def narrow(x):
        rows = jnp.stack([x[:, r * L : (r + 1) * L] for r in range(R)], axis=0)
        return jnp.swapaxes(rows, 0, 1)

    solution_ref[...] = narrow(found)
    residual_ref[...] = narrow(left_over)
    sent(0)
    sent(1)
    for copy in ec + es + lc + ls:
        copy.wait_send()


def body(n, N, right_side, stiff_scale, extra_diag, iface_line, partner):
    C, R, L = right_side.shape
    slots = iface_line.shape[0]
    vmem = pl.BlockSpec(memory_space=pltpu.VMEM)
    hbm = pl.BlockSpec(memory_space=pltpu.HBM)
    dma = pltpu.SemaphoreType.DMA
    field = pltpu.VMEM((C, R, L), F32)
    return pl.pallas_call(
        functools.partial(kernel, n, N),
        out_shape=(field, field),
        in_specs=[hbm] * 5,
        out_specs=(vmem, vmem),
        scratch_shapes=[
            pltpu.VMEM((C, R, L), F32),
            pltpu.VMEM((R, L), F32),
            pltpu.VMEM((R, L), F32),
            pltpu.SMEM((slots,), jnp.int32),
            pltpu.SMEM((slots,), jnp.int32),
            pltpu.VMEM((3, R, C, L), F32),
            pltpu.VMEM((2, R, C, L), F32),
            pltpu.VMEM((3, R, 3 * C, L), jnp.bfloat16),
            pltpu.VMEM((R * C, 4 * L), jnp.bfloat16),
            pltpu.VMEM((2, TILE, R * C), F32),
            pltpu.VMEM((2, 2 * TILE, R * C), F32),
            pltpu.VMEM((2, n * slots, R * C), F32),
            pltpu.VMEM((2, 2, REACH, C, L), F32),
            pltpu.VMEM((2, 2, 2 * TILE, LANES), F32),
            pltpu.VMEM((R + 2 * REACH, C, L), F32),
            pltpu.VMEM((R + 2 * REACH, C, L), F32),
            pltpu.VMEM((n, C, LANES), F32),
            pltpu.VMEM((N, C, LANES), F32),
            pltpu.VMEM((n, C, LANES), F32),
            pltpu.VMEM((N, C, LANES), F32),
            dma((2, 2, 2)),
            dma((2, 2, 2)),
            dma((2, 2, 2, 2)),
            dma((2, 2, n)),
            dma((2, 2, n)),
            dma((2, 2, N)),
            dma((5,)),
        ],
        compiler_params=pltpu.CompilerParams(
            collective_id=0, has_side_effects=True, vmem_limit_bytes=60 * 1024 * 1024
        ),
        name="shell_cg",
    )(right_side, stiff_scale, extra_diag, iface_line, partner)


def solution(mesh):
    sizes = dict(mesh.shape)
    return jax.shard_map(
        functools.partial(body, sizes["chord"], sizes["span"]),
        mesh=mesh,
        in_specs=(
            P(None, "span", "chord"),
            P("span", "chord"),
            P("span", "chord"),
            P("chord"),
            P("chord"),
        ),
        out_specs=(P(None, "span", "chord"), P(None, "span", "chord")),
        check_vma=False,
    )
```

```python
import functools

import jax
import jax.numpy as jnp
from jax import lax
from jax.experimental import pallas as pl
from jax.experimental.pallas import tpu as pltpu
from jax.sharding import PartitionSpec as P

mass_taps = (1.0, 120.0, 1191.0, 2416.0, 1191.0, 120.0, 1.0)
mass_high = (1.0, 120.0, 1192.0, 2416.0, 1192.0, 120.0, 1.0)
mass_low = (0.0, 0.0, -1.0, 0.0, -1.0, 0.0, 0.0)
bend_taps = (1.0, 0.0, -9.0, 16.0, -9.0, 0.0, 1.0)
tap_unit = 1.0 / (5040.0 * 6.0)
penalty_weight = 4.0
REACH = 3
LANES = 128
TILE = 8
F32 = jnp.float32
MESH = pl.DeviceIdType.MESH


def dot(a, b, a_dim, b_dim, precision=lax.Precision.HIGH):
    return lax.dot_general(
        a,
        b,
        (((a_dim,), (b_dim,)), ((), ())),
        precision=precision,
        preferred_element_type=F32,
    )


def product(a, b, a_dim, b_dim):
    return lax.dot_general(a, b, (((a_dim,), (b_dim,)), ((), ())), preferred_element_type=F32)


def split(x):
    high = x.astype(jnp.bfloat16)
    rest = x - high.astype(F32)
    mid = rest.astype(jnp.bfloat16)
    low = (rest - mid.astype(F32)).astype(jnp.bfloat16)
    return high, mid, low


exact_dot = functools.partial(dot, precision=lax.Precision.HIGHEST)


def iota(shape, dim):
    return lax.broadcasted_iota(jnp.int32, shape, dim)


def taps_at(offset, taps):
    out = jnp.zeros(offset.shape, F32)
    for o in range(-REACH, REACH + 1):
        if taps[o + REACH] != 0.0:
            out = jnp.where(offset == o, F32(taps[o + REACH]), out)
    return out


def span_sum(ext_ref, taps, rows):
    total = F32(taps[REACH]) * ext_ref[REACH : REACH + rows]
    for o in range(1, REACH + 1):
        if taps[REACH + o] != 0.0:
            pair = ext_ref[REACH - o : REACH - o + rows] + ext_ref[REACH + o : REACH + o + rows]
            total = total + F32(taps[REACH + o]) * pair
    return total


def eliminate(table, first, count):
    row_at = iota(table.shape, 0)
    columns = [
        jnp.broadcast_to(table[:, first + k : first + k + 1], table.shape) for k in range(count)
    ]
    for k in range(count):
        factor = columns[k]
        inverse = 1.0 / factor[k : k + 1, :]

        def reduce(x):
            row = x[k : k + 1, :] * inverse
            return jnp.where(row_at == k, row, x - factor * row)

        table = reduce(table)
        for j in range(k + 1, count):
            columns[j] = reduce(columns[j])
    return table


def kernel(
    n,
    N,
    right_hbm,
    scale_hbm,
    extra_hbm,
    line_hbm,
    partner_hbm,
    solution_ref,
    residual_ref,
    right_ref,
    scale_ref,
    extra_ref,
    line_ref,
    partner_ref,
    basis,
    weighted,
    terms,
    w_terms,
    halo_out,
    halo,
    iface,
    rim,
    corner,
    ext_m,
    ext_b,
    early_c,
    early_s,
    late_c,
    late_s,
    rim_sems,
    halo_sems,
    corner_sems,
    iface_sems,
    chord_sems,
    span_sems,
    load_sems,
):
    C, R, L = right_ref.shape
    RC = R * C
    slots = line_ref.shape[0]
    s = lax.axis_index("span")
    c = lax.axis_index("chord")
    right, left = lax.rem(c + 1, n), lax.rem(c + n - 1, n)
    above, below = s > 0, s < N - 1

    loads = [
        pltpu.make_async_copy(src, dst, load_sems.at[k])
        for k, (src, dst) in enumerate(
            (
                (right_hbm, right_ref),
                (scale_hbm, scale_ref),
                (extra_hbm, extra_ref),
                (line_hbm, line_ref),
                (partner_hbm, partner_ref),
            )
        )
    ]
    for load in loads:
        load.start()

    barrier = pltpu.get_barrier_semaphore()
    for d in range(1, n):
        pl.semaphore_signal(barrier, inc=1, device_id=(s, lax.rem(c + d, n)), device_id_type=MESH)
    for d in range(1, N):
        pl.semaphore_signal(barrier, inc=1, device_id=(lax.rem(s + d, N), c), device_id_type=MESH)

    @pl.when(above)
    def _():
        for side in (left, right):
            pl.semaphore_signal(barrier, inc=1, device_id=(s - 1, side), device_id_type=MESH)

    @pl.when(below)
    def _():
        for side in (left, right):
            pl.semaphore_signal(barrier, inc=1, device_id=(s + 1, side), device_id_type=MESH)

    @pl.when(jnp.logical_not(above))
    def _():
        for t in range(2):
            rim[t, 0] = jnp.zeros(rim.shape[2:], F32)
            corner[t, 0] = jnp.zeros(corner.shape[2:], F32)

    @pl.when(jnp.logical_not(below))
    def _():
        for t in range(2):
            rim[t, 1] = jnp.zeros(rim.shape[2:], F32)
            corner[t, 1] = jnp.zeros(corner.shape[2:], F32)

    offset = iota((L, L), 0) - iota((L, L), 1)

    def bands(at):
        bend = taps_at(at, bend_taps)
        high = jnp.concatenate([taps_at(at, mass_high), bend], axis=1)
        low = jnp.concatenate([taps_at(at, mass_low), jnp.zeros_like(bend)], axis=1)
        return jnp.concatenate([high, high, high, low], axis=0).astype(jnp.bfloat16)

    band = bands(offset)
    k_at, c_at = iota((2 * TILE, L), 0), iota((2 * TILE, L), 1)
    from_left = jnp.logical_and(k_at >= REACH, k_at < 2 * REACH)
    from_right = jnp.logical_and(k_at >= TILE, k_at < TILE + REACH)
    place = jnp.where(k_at < TILE, k_at - 2 * REACH, L + k_at - TILE)
    reach = jnp.where(jnp.logical_or(from_left, from_right), place - c_at, 2 * L)
    side_band = bands(reach)
    h_at, hc_at = iota((2 * TILE, L), 0), iota((2 * TILE, L), 1)
    halo_line = jnp.where(h_at < REACH, h_at, L - 2 * REACH + h_at)
    halo_pick = jnp.where(
        jnp.logical_and(h_at < 2 * REACH, halo_line == hc_at), F32(1.0), F32(0.0)
    )

    for load in loads:
        load.wait()

    halo_pick = jnp.concatenate([halo_pick] * 3, axis=1).astype(jnp.bfloat16)

    q_at, qc_at = iota((2 * TILE, L), 0), iota((2 * TILE, L), 1)
    j_at, jc_at = iota((n * slots, L), 0), iota((n * slots, L), 1)
    pick = jnp.zeros((2 * TILE, L), F32)
    spread = jnp.zeros((n * slots, L), F32)
    for q in range(slots):
        line, mate = line_ref[q], partner_ref[q]
        pick = jnp.where(jnp.logical_and(q_at == q, qc_at == line), F32(1.0), pick)
        owner = lax.div(mate, jnp.int32(slots))
        away = c - owner
        away = jnp.where(away < 0, away + n, away)
        at = away * slots + (mate - owner * slots)
        spread = jnp.where(jnp.logical_and(j_at == at, jc_at == line), F32(-penalty_weight), spread)
    on_line = jnp.sum(pick, axis=0, keepdims=True)
    pick = jnp.concatenate([pick] * 3, axis=1).astype(jnp.bfloat16)
    spread = jnp.concatenate([spread] * 3, axis=0).astype(jnp.bfloat16)

    scale = scale_ref[...][:, None, :]
    diag = (extra_ref[...] + F32(penalty_weight) * on_line)[:, None, :]

    def remote(src, dst, sems, at, to):
        return pltpu.make_async_remote_copy(
            src_ref=src,
            dst_ref=dst,
            send_sem=sems.at[(0,) + at],
            recv_sem=sems.at[(1,) + at],
            device_id=to,
            device_id_type=MESH,
        )

    def keep(t, field):
        basis[t] = field
        for k, term in enumerate(split(field)):
            terms[t, :, k * C : (k + 1) * C] = term

    def wide(t, count=3):
        return jnp.concatenate([terms[t, r, 0 : count * C] for r in range(R)], axis=1)

    def stacked(x, axis):
        high, mid, low = split(x)
        return jnp.concatenate([high, mid, low, high], axis=axis)

    def copies(t):
        down = [remote(weighted.at[t, pl.ds(R - REACH, REACH)], rim.at[t, 0], rim_sems, (t, 0), (s + 1, c))]
        up = [remote(weighted.at[t, pl.ds(0, REACH)], rim.at[t, 1], rim_sems, (t, 1), (s - 1, c))]
        last, first = pl.ds(RC - LANES, LANES), pl.ds(0, LANES)
        for k, to in enumerate((right, left)):
            spot = pl.ds(k * TILE, TILE)
            down.append(
                remote(halo_out.at[t, :, last], corner.at[t, 0, spot], corner_sems, (t, 0, k), (s + 1, to))
            )
            up.append(
                remote(halo_out.at[t, :, first], corner.at[t, 1, spot], corner_sems, (t, 1, k), (s - 1, to))
            )
        around = []
        for k, to in enumerate((right, left)):
            spot = pl.ds(k * TILE, TILE)
            around.append(remote(halo_out.at[t], halo.at[t, spot], halo_sems, (t, k), (s, to)))
        lines = []
        for d in range(1, n):
            lines.append(
                remote(
                    iface.at[t, pl.ds(0, slots)],
                    iface.at[t, pl.ds(d * slots, slots)],
                    iface_sems,
                    (t, d),
                    (s, lax.rem(c + d, n)),
                )
            )
        return down, up, around, lines

    def prepare(t):
        w = scale * basis[t]
        weighted[t] = w
        w_terms[...] = stacked(w.reshape(RC, L), 1)
        halo_out[t] = product(halo_pick, w_terms[:, 0 : 3 * L], 1, 1)[:TILE]

    def prepare_lines(t):
        v = jnp.concatenate(
            [terms[t, :, k * C : (k + 1) * C].reshape(RC, L) for k in range(3)], axis=1
        )
        iface[t, 0:slots] = product(pick, v, 1, 1)[:slots]

    def send(t):
        down, up, around, lines = copies(t)

        @pl.when(below)
        def _():
            for copy in down:
                copy.start()

        @pl.when(above)
        def _():
            for copy in up:
                copy.start()

        for copy in around:
            copy.start()
        prepare_lines(t)
        for copy in lines:
            copy.start()

    def inner():
        both = product(w_terms[...], band, 1, 0)
        ext_m[REACH : REACH + R] = both[:, :L].reshape(R, C, L)
        ext_b[REACH : REACH + R] = both[:, L:].reshape(R, C, L)

    def sent(t):
        down, up, around, lines = copies(t)

        @pl.when(below)
        def _():
            for copy in down:
                copy.wait_send()

        @pl.when(above)
        def _():
            for copy in up:
                copy.wait_send()

        for copy in around + lines:
            copy.wait_send()

    def outer(t):
        down, up, around, lines = copies(t)

        @pl.when(above)
        def _():
            for copy in down:
                copy.wait_recv()

        @pl.when(below)
        def _():
            for copy in up:
                copy.wait_recv()

        edge = REACH * C
        ends = product(stacked(rim[t].reshape(2 * edge, L), 1), band, 1, 0)
        top = ends[:edge] + product(stacked(corner[t, 0], 0), side_band, 0, 0)[LANES - edge :]
        low = ends[edge:] + product(stacked(corner[t, 1], 0), side_band, 0, 0)[:edge]
        ext_m[0:REACH] = top[:, :L].reshape(REACH, C, L)
        ext_b[0:REACH] = top[:, L:].reshape(REACH, C, L)
        ext_m[REACH + R :] = low[:, :L].reshape(REACH, C, L)
        ext_b[REACH + R :] = low[:, L:].reshape(REACH, C, L)
        for copy in around:
            copy.wait_recv()
        mid = product(stacked(halo[t], 0), side_band, 0, 0)
        ext_m[REACH : REACH + R] += mid[:, :L].reshape(R, C, L)
        ext_b[REACH : REACH + R] += mid[:, L:].reshape(R, C, L)
        y = span_sum(ext_m, bend_taps, R) + span_sum(ext_b, mass_taps, R)
        for copy in lines:
            copy.wait_recv()
        every = jnp.concatenate(split(iface[t]), axis=0)
        coupled = product(every, spread, 0, 0).reshape(R, C, L)
        keep(t + 1, (scale * F32(tap_unit)) * y + diag * basis[t] + coupled)

    def group_copies(buf, sems, which, count, to):
        return [remote(buf.at[0], buf.at[d], sems, (which, d), to(d)) for d in range(1, count)]

    def along_chord(d):
        return (s, lax.rem(c + d, n))

    def along_span(d):
        return (lax.rem(s + d, N), c)

    def total(buf, count):
        out = buf[0]
        for d in range(1, count):
            out = out + buf[d]
        return out

    def pad(x):
        return jnp.concatenate([x, jnp.zeros((x.shape[0], LANES - x.shape[1]), F32)], axis=1)

    ec = group_copies(early_c, chord_sems, 0, n, along_chord)
    es = group_copies(early_s, span_sems, 0, N, along_span)
    lc = group_copies(late_c, chord_sems, 1, n, along_chord)
    ls = group_copies(late_s, span_sems, 1, N, along_span)

    def gram(table, i, j):
        block = table[3 * C * i : 3 * C * (i + 1), 3 * C * j : 3 * C * (j + 1)]
        rows = block[:C] + block[C : 2 * C] + block[2 * C :]
        return rows[:, :C] + rows[:, C : 2 * C] + rows[:, 2 * C :]

    keep(0, jnp.swapaxes(right_ref[...], 0, 1))
    greeted = (n - 1) + (N - 1) + 2 * (above.astype(jnp.int32) + below.astype(jnp.int32))

    @pl.loop(0, 2)
    def _(t):
        prepare(t)

        @pl.when(t == 0)
        def _():
            pl.semaphore_wait(barrier, greeted)

        send(t)

        @pl.when(t == 1)
        def _():
            pair = jnp.concatenate([wide(0), wide(1)], axis=0)
            early = product(pair, pair, 1, 1)
            early_c[0] = pad(
                jnp.concatenate([gram(early, 0, 1), gram(early, 1, 1), gram(early, 0, 0)], axis=1)
            )
            for copy in ec:
                copy.start()

        inner()

        @pl.when(t == 1)
        def _():
            for copy in ec:
                copy.wait_recv()
            early_s[0] = total(early_c, n)
            for copy in es:
                copy.start()

        outer(t)

    late = gram(product(wide(1), wide(2), 1, 1), 0, 0)
    late_c[0] = pad(jnp.concatenate([jnp.zeros((C, C), F32), late], axis=1))
    for copy in lc:
        copy.start()
    for copy in es:
        copy.wait_recv()
    table = total(early_s, N)
    g01, g11 = table[:, :C], table[:, C : 2 * C]
    table = eliminate(table, 0, C)
    for copy in lc:
        copy.wait_recv()
    late_s[0] = total(late_c, n)
    for copy in ls:
        copy.start()
    folded = exact_dot(g11, table, 1, 0)
    slope = table[:, C : 2 * C]
    step = table[:, 2 * C : 3 * C]
    lead = pad(jnp.concatenate([jnp.zeros((C, 2 * C), F32), g01], axis=1))
    rest = lead - folded
    for copy in ls:
        copy.wait_recv()
    table = eliminate(rest + total(late_s, N), C, C)
    y1 = table[:, 2 * C : 3 * C]
    y0 = step - exact_dot(slope, y1, 1, 0)
    (a0, b0, c0), (a1, b1, c1) = split(y0), split(y1)
    mix = jnp.concatenate([a0, a0, a0, a1, a1, a1, b0, b0, b1, b1, c0, c1], axis=0)

    def mixed(i, j):
        field = jnp.concatenate(
            [wide(i), wide(j), wide(i, 2), wide(j, 2), wide(i, 1), wide(j, 1)], axis=0
        )
        return product(mix, field, 0, 0)

    found = mixed(0, 1)
    start = jnp.concatenate([basis[0, r] for r in range(R)], axis=1)
    left_over = start - mixed(1, 2)

    def narrow(x):
        rows = jnp.stack([x[:, r * L : (r + 1) * L] for r in range(R)], axis=0)
        return jnp.swapaxes(rows, 0, 1)

    solution_ref[...] = narrow(found)
    residual_ref[...] = narrow(left_over)
    sent(0)
    sent(1)
    for copy in ec + es + lc + ls:
        copy.wait_send()


def body(n, N, right_side, stiff_scale, extra_diag, iface_line, partner):
    C, R, L = right_side.shape
    slots = iface_line.shape[0]
    vmem = pl.BlockSpec(memory_space=pltpu.VMEM)
    hbm = pl.BlockSpec(memory_space=pltpu.HBM)
    dma = pltpu.SemaphoreType.DMA
    field = pltpu.VMEM((C, R, L), F32)
    return pl.pallas_call(
        functools.partial(kernel, n, N),
        out_shape=(field, field),
        in_specs=[hbm] * 5,
        out_specs=(vmem, vmem),
        scratch_shapes=[
            pltpu.VMEM((C, R, L), F32),
            pltpu.VMEM((R, L), F32),
            pltpu.VMEM((R, L), F32),
            pltpu.SMEM((slots,), jnp.int32),
            pltpu.SMEM((slots,), jnp.int32),
            pltpu.VMEM((3, R, C, L), F32),
            pltpu.VMEM((2, R, C, L), F32),
            pltpu.VMEM((3, R, 3 * C, L), jnp.bfloat16),
            pltpu.VMEM((R * C, 4 * L), jnp.bfloat16),
            pltpu.VMEM((2, TILE, R * C), F32),
            pltpu.VMEM((2, 2 * TILE, R * C), F32),
            pltpu.VMEM((2, n * slots, R * C), F32),
            pltpu.VMEM((2, 2, REACH, C, L), F32),
            pltpu.VMEM((2, 2, 2 * TILE, LANES), F32),
            pltpu.VMEM((R + 2 * REACH, C, L), F32),
            pltpu.VMEM((R + 2 * REACH, C, L), F32),
            pltpu.VMEM((n, C, LANES), F32),
            pltpu.VMEM((N, C, LANES), F32),
            pltpu.VMEM((n, C, LANES), F32),
            pltpu.VMEM((N, C, LANES), F32),
            dma((2, 2, 2)),
            dma((2, 2, 2)),
            dma((2, 2, 2, 2)),
            dma((2, 2, n)),
            dma((2, 2, n)),
            dma((2, 2, N)),
            dma((5,)),
        ],
        compiler_params=pltpu.CompilerParams(
            collective_id=0, has_side_effects=True, vmem_limit_bytes=60 * 1024 * 1024
        ),
        name="shell_cg",
    )(right_side, stiff_scale, extra_diag, iface_line, partner)


def solution(mesh):
    sizes = dict(mesh.shape)
    return jax.shard_map(
        functools.partial(body, sizes["chord"], sizes["span"]),
        mesh=mesh,
        in_specs=(
            P(None, "span", "chord"),
            P("span", "chord"),
            P("span", "chord"),
            P("chord"),
            P("chord"),
        ),
        out_specs=(P(None, "span", "chord"), P(None, "span", "chord")),
        check_vma=False,
    )
```
